256 devices in a mesh: section: 16 (over y_hi, z), tensor: 4 (over x), dp: 4 (over y_lo, core).
Axes of the slice: x: 4, y: 4 (y_hi: 2, y_lo: 2; y = y_hi * 2 + y_lo), z: 8, core: 2. Of those that a mesh axis runs over, the one named last changes fastest.
Arguments:
- inbound: bfloat16 [16, 4, 3, 384, 6144], P('section', 'dp', None, None, 'tensor'), may hold values from -6 to 6
- parked: bfloat16 [16, 4, 3, 384, 6144], P('section', 'dp', None, None, 'tensor'), may hold values from -6 to 6
- grad_out: bfloat16 [16, 4, 384, 6144], P('section', 'dp', None, 'tensor'), may hold values from -6 to 6
- query_gain: float32 [16, 6144], P('section', 'tensor'), may hold values from 0.5 to 1.5
- plan: int32 [16, 2], P('section'), may hold values from 0 to 7
- lengths: int32 [4, 8], P('dp'), may hold values from 1 to 384
Outputs:
- attended: bfloat16 [16, 4, 384, 6144], P('section', 'dp', None, 'tensor')
- grads_qkv: bfloat16 [16, 4, 3, 384, 6144], P('section', 'dp', None, None, 'tensor')
- gain_grad: float32 [16, 6144], P('section', 'tensor')
The draws below stay inside these ranges and needn't reach their ends.
All inputs are finite; a program needn't handle non-finite values.
Results may differ from the reference program's by a relative error of at most 0.022.
Values may be sent and summed in bfloat16 or wider, within the bound.
No kernel may reach another device: no remote copies, remote signals or barrier semaphores. Data moves between devices by JAX's collectives and lax.ppermute only.
A program may use at most 128 MiB of HBM per device.

```python
import jax
import jax.numpy as jnp
from jax import lax

HEADS = 48
HD = 128
SEQ = 384
MBS = 8
N_SECTION = 16
N_DP = 4


def draw_inbound(key, part):
    key = jax.random.fold_in(key, 11)
    array_shape = (N_SECTION, N_DP, 3, SEQ, HEADS * HD)
    result = jnp.clip(jax.random.normal(key, array_shape, jnp.float32), -6.0, 6.0)
    return result.astype(jnp.bfloat16)


def draw_parked(key, part):
    key = jax.random.fold_in(key, 23)
    array_shape = (N_SECTION, N_DP, 3, SEQ, HEADS * HD)
    result = jnp.clip(jax.random.normal(key, array_shape, jnp.float32), -6.0, 6.0)
    return result.astype(jnp.bfloat16)


def plant(values, own_key, smallest, top_value):
    extent = values.shape
    spot = [jax.random.randint(jax.random.fold_in(own_key, axis), (), 0, extent[axis]) for axis in range(len(extent))]
    values = values.at[tuple(spot)].set(smallest)
    longest = extent.index(max(extent))
    spot[longest] = (spot[longest] + 1) % extent[longest]
    return values.at[tuple(spot)].set(top_value)


def shard_levels(own_key, extent, shards, low, top_value):
    def one(dim, blocks):
        heights = jax.random.uniform(jax.random.fold_in(jax.random.fold_in(own_key, 6), dim), (blocks,), jnp.float32, low / len(shards), top_value / len(shards))
        return jnp.repeat(jnp.exp(heights), extent[dim] // blocks).reshape((-1,) + (1,) * (len(extent) - dim - 1))

    factor_of = one(*shards[0])
    for cut in shards[1:]:
        factor_of = factor_of * one(*cut)
    return factor_of


def centred(own_key, extent, deviation, limit, cuts=(), kind=jnp.bfloat16):
    values = jax.random.normal(own_key, extent, jnp.float32) * deviation
    if len(cuts) > 0:
        values = shard_levels(own_key, extent, cuts, -0.22, 0.18) * values
    return jnp.clip(values, min=-limit, max=limit).astype(kind)


def setup_inputs(seed: int = 0) -> dict:
    key_list = jax.random.split(jax.random.key(seed), 7)
    inbound = draw_inbound(jax.random.fold_in(key_list[6], 71), 0)
    parked = draw_parked(jax.random.fold_in(key_list[6], 71), 0)
    grad_out = centred(key_list[2], (N_SECTION, N_DP, SEQ, HEADS * HD), 1.0, 6.0, ((0, 16), (1, 4), (3, 4)))
    query_gain = jnp.clip(1.0 + 0.1 * jax.random.normal(key_list[3], (N_SECTION, HEADS * HD), jnp.float32), 0.5, 1.5)
    plan = plant(jax.random.randint(key_list[4], (N_SECTION, 2), 0, MBS), jax.random.fold_in(key_list[4], 1), 0, MBS - 1).astype(jnp.int32)
    lengths = plant(jax.random.randint(key_list[5], (N_DP, MBS), 1, SEQ + 1), jax.random.fold_in(key_list[5], 1), 1, SEQ).astype(jnp.int32)
    return {"inbound": inbound, "parked": parked, "grad_out": grad_out, "query_gain": query_gain, "plan": plan, "lengths": lengths}


def masked_weights(query, keys, length):
    seq = query.shape[0]
    heads = query.shape[1] // HD
    qh = query.reshape(seq, heads, HD).astype(jnp.float32)
    kh = keys.reshape(seq, heads, HD).astype(jnp.float32)
    scores = jnp.einsum('qhd,khd->hqk', qh, kh) / jnp.sqrt(jnp.float32(HD))
    rows = jnp.arange(seq)[:, None]
    cols = jnp.arange(seq)[None, :]
    allowed = (cols <= rows) & (cols < length)
    scores = jnp.where(allowed[None], scores, jnp.float32(-1e+30))
    top = lax.optimization_barrier(jnp.max(scores, axis=-1, keepdims=True))
    expo = jnp.exp(scores - top)
    return expo / lax.optimization_barrier(jnp.sum(expo, axis=-1, keepdims=True))

def forward_part(query, keys, values, gain, length):
    seq = query.shape[0]
    heads = query.shape[1] // HD
    scaled = (query.astype(jnp.float32) * gain).astype(jnp.bfloat16)
    weights = masked_weights(scaled, keys, length).astype(jnp.bfloat16)
    vh = values.reshape(seq, heads, HD).astype(jnp.float32)
    out = jnp.einsum('hqk,khd->qhd', weights.astype(jnp.float32), vh)
    return out.reshape(seq, heads * HD).astype(jnp.bfloat16)

def backward_part(query, keys, values, upstream, gain, length):
    seq = query.shape[0]
    heads = query.shape[1] // HD
    scaled = (query.astype(jnp.float32) * gain).astype(jnp.bfloat16)
    weights = masked_weights(scaled, keys, length)
    wround = weights.astype(jnp.bfloat16).astype(jnp.float32)
    gh = upstream.reshape(seq, heads, HD).astype(jnp.float32)
    vh = values.reshape(seq, heads, HD).astype(jnp.float32)
    kh = keys.reshape(seq, heads, HD).astype(jnp.float32)
    sh = scaled.reshape(seq, heads, HD).astype(jnp.float32)
    dvalue = jnp.einsum('hqk,qhd->khd', wround, gh)
    recomputed = jnp.einsum('hqk,khd->qhd', wround, vh)
    dweight = jnp.einsum('qhd,khd->hqk', gh, vh)
    delta = jnp.einsum('qhd,qhd->hq', gh, recomputed)
    dscore = (weights * (dweight - delta[:, :, None]) / jnp.sqrt(jnp.float32(HD))).astype(jnp.bfloat16).astype(jnp.float32)
    dscaled = jnp.einsum('hqk,khd->qhd', dscore, kh).reshape(seq, heads * HD)
    dkeys = jnp.einsum('hqk,qhd->khd', dscore, sh).reshape(seq, heads * HD)
    dquery = dscaled * gain
    raw = lax.optimization_barrier(jnp.sum(dscaled * query.astype(jnp.float32), axis=0))
    stacked = jnp.stack([dquery, dkeys, dvalue.reshape(seq, heads * HD)]).astype(jnp.bfloat16)
    return (stacked, raw)

def reference(inbound, parked, grad_out, query_gain, plan, lengths):
    outs = []
    grads = []
    raws = []
    for section in range(N_SECTION):
        previous = (section - 1) % N_SECTION
        following = (section + 1) % N_SECTION
        mirror = N_SECTION - 1 - section
        gain = query_gain[section]
        row_out = []
        row_grad = []
        raw = jnp.zeros((query_gain.shape[1],), jnp.float32)
        for replica in range(N_DP):
            flen = lengths[replica, plan[section, 0]]
            blen = lengths[replica, plan[section, 1]]
            block = inbound[previous, replica]
            row_out.append(forward_part(block[0], block[1], block[2], gain, flen))
            stored = parked[mirror, replica]
            stacked, part = backward_part(stored[0], stored[1], stored[2], grad_out[following, replica], gain, blen)
            row_grad.append(stacked)
            raw = raw + part
        outs.append(jnp.stack(row_out))
        grads.append(jnp.stack(row_grad))
        raws.append(raw)
    raw_all = jnp.stack(raws)
    norm = jnp.sqrt(jnp.sum(raw_all * raw_all)) + 1e-06
    return (jnp.stack(outs), jnp.stack(grads), raw_all / norm)
```

```python
import functools

import jax
import jax.numpy as jnp
from jax import lax
from jax.experimental import pallas as pl
from jax.experimental.pallas import tpu as pltpu
from jax.sharding import PartitionSpec as P

HD = 128
BLOCK = 128
HEADS_PER_STEP = 2
STRIPS = 4
NEG = -1e30

DIM_LAST = (((1,), (1,)), ((), ()))
DIM_FIRST = (((0,), (0,)), ((), ()))


def site(s, n):
    return s if s % (n // 2) in (1, 2, 5, 6) else n - 1 - s


def moved(value, target):
    size = lax.axis_size("section")
    return lax.ppermute(value, "section", [(i, target(i, size) % size) for i in range(size)])


def doubled_sum(value, axis):
    size = lax.axis_size(axis)
    step = 1
    while step < size:
        value = value + lax.ppermute(value, axis, [(i, i ^ step) for i in range(size)])
        step *= 2
    return value


def dot(a, b, dims=(((1,), (0,)), ((), ()))):
    return lax.dot_general(a, b, dims, preferred_element_type=jnp.float32)


def row_length(tail_ref, lengths_ref, column):
    index = tail_ref[:, column : column + 1].astype(jnp.int32)
    table = lengths_ref[...]
    lanes = lax.broadcasted_iota(jnp.int32, table.shape, 1)
    return jnp.sum(jnp.where(lanes == index, table, 0), axis=1, keepdims=True)


def weights_of(qs, keys, start, length):
    n = keys.shape[0]
    scores = dot(keys, qs, DIM_LAST) * (1.0 / HD**0.5)
    rows = lax.broadcasted_iota(jnp.int32, scores.shape, 0)
    cols = lax.broadcasted_iota(jnp.int32, scores.shape, 1) + start
    scores = jnp.where((rows <= cols) & (rows < length), scores, NEG)
    top = jnp.max(scores, axis=0, keepdims=True)
    expo = jnp.exp(scores - top)
    return expo * (1.0 / jnp.sum(expo, axis=0, keepdims=True))


def forward_kernel(q_ref, k_ref, v_ref, gain_ref, tail_ref, lengths_ref, out_ref):
    length = row_length(tail_ref, lengths_ref, 0)
    seq = q_ref.shape[0]
    for h in range(HEADS_PER_STEP):
        hs = slice(h * HD, (h + 1) * HD)
        gain = gain_ref[:, hs]
        for start in range(0, seq, BLOCK):
            end = start + BLOCK
            qs = (q_ref[start:end, hs].astype(jnp.float32) * gain).astype(jnp.bfloat16)
            wb = weights_of(qs, k_ref[:end, hs], start, length).astype(jnp.bfloat16)
            out_ref[start:end, hs] = dot(wb, v_ref[:end, hs], DIM_FIRST).astype(jnp.bfloat16)


def backward_kernel(*refs):
    strips = refs[:STRIPS]
    g_ref, gain_ref, tail_ref, lengths_ref, out_ref, raw_ref = refs[STRIPS:]
    length = row_length(tail_ref, lengths_ref, 1)
    seq = g_ref.shape[0]
    for h in range(HEADS_PER_STEP):
        hs = slice(h * HD, (h + 1) * HD)
        gain = gain_ref[:, hs]
        q, k, v = (jnp.concatenate([strip[part, :, hs] for strip in strips], axis=0) for part in range(3))
        dks = [jnp.zeros((BLOCK, HD), jnp.float32) for _ in range(seq // BLOCK)]
        dvs = [jnp.zeros((BLOCK, HD), jnp.float32) for _ in range(seq // BLOCK)]
        raw = jnp.zeros((1, HD), jnp.float32)
        for start in range(0, seq, BLOCK):
            end = start + BLOCK
            query = q[start:end].astype(jnp.float32)
            qs = (query * gain).astype(jnp.bfloat16)
            keys = k[:end]
            g = g_ref[start:end, hs]
            w = weights_of(qs, keys, start, length)
            wb = w.astype(jnp.bfloat16)
            dw = dot(v[:end], g, DIM_LAST)
            delta = jnp.sum(wb.astype(jnp.float32) * dw, axis=0, keepdims=True)
            ds = (w * (dw - delta) * (1.0 / HD**0.5)).astype(jnp.bfloat16)
            dv = dot(wb, g)
            dk = dot(ds, qs)
            for b in range(end // BLOCK):
                dvs[b] = dvs[b] + dv[b * BLOCK : (b + 1) * BLOCK]
                dks[b] = dks[b] + dk[b * BLOCK : (b + 1) * BLOCK]
            dqs = dot(ds, keys, DIM_FIRST)
            out_ref[0, start:end, hs] = (dqs * gain).astype(jnp.bfloat16)
            raw = raw + jnp.sum(dqs * query, axis=0, keepdims=True)
        for b in range(seq // BLOCK):
            out_ref[1, b * BLOCK : (b + 1) * BLOCK, hs] = dks[b].astype(jnp.bfloat16)
            out_ref[2, b * BLOCK : (b + 1) * BLOCK, hs] = dvs[b].astype(jnp.bfloat16)
        raw_ref[:, hs] = raw


def qkv_specs(seq, width):
    return [
        pl.BlockSpec((None, None, None, seq, width), functools.partial(lambda h, part: (0, 0, part, 0, h), part=part))
        for part in range(3)
    ]


def small_specs(width, features, table):
    return [
        pl.BlockSpec((1, width), lambda h: (0, h)),
        pl.BlockSpec((1, HD), lambda h: (0, features // HD)),
        pl.BlockSpec(table.shape, lambda h: (0, 0)),
    ]


def forward_part(block, aux, lengths):
    seq, features = block.shape[3:]
    width = HEADS_PER_STEP * HD
    heads = features // HD
    return pl.pallas_call(
        forward_kernel,
        grid=(features // width,),
        in_specs=[*qkv_specs(seq, width), *small_specs(width, features, lengths)],
        out_specs=pl.BlockSpec((None, None, seq, width), lambda h: (0, 0, 0, h)),
        out_shape=jax.ShapeDtypeStruct((1, 1, seq, features), jnp.bfloat16),
        cost_estimate=pl.CostEstimate(
            flops=4 * heads * seq * seq * HD, bytes_accessed=8 * seq * features, transcendentals=heads * seq * seq
        ),
        name="forward",
    )(block, block, block, aux, aux, lengths)


def backward_part(strips, upstream, aux, lengths):
    seq, features = upstream.shape[2:]
    rows = seq // STRIPS
    width = HEADS_PER_STEP * HD
    heads = features // HD
    return pl.pallas_call(
        backward_kernel,
        grid=(features // width,),
        in_specs=[
            *[pl.BlockSpec((None, None, 3, rows, width), lambda h: (0, 0, 0, 0, h))] * STRIPS,
            pl.BlockSpec((None, None, seq, width), lambda h: (0, 0, 0, h)),
            *small_specs(width, features, lengths),
        ],
        out_specs=[
            pl.BlockSpec((None, None, 3, seq, width), lambda h: (0, 0, 0, 0, h)),
            pl.BlockSpec((1, width), lambda h: (0, h)),
        ],
        out_shape=[
            jax.ShapeDtypeStruct((1, 1, 3, seq, features), jnp.bfloat16),
            jax.ShapeDtypeStruct((1, features), jnp.float32),
        ],
        cost_estimate=pl.CostEstimate(
            flops=10 * heads * seq * seq * HD, bytes_accessed=14 * seq * features, transcendentals=heads * seq * seq
        ),
        name="backward",
    )(*strips, upstream, aux, aux, lengths)


def shards(inbound, parked, grad_out, query_gain, plan, lengths):
    entries = plan.shape[1]
    aux = jnp.concatenate(
        [query_gain, plan.astype(jnp.float32), jnp.zeros((1, HD - entries), jnp.float32)], axis=1
    )
    aux_back = moved(aux, lambda s, n: site(s, n))
    aux_ahead = moved(aux, lambda s, n: s - 1)
    grad_out, parked, aux_back, aux_ahead = lax.optimization_barrier((grad_out, parked, aux_back, aux_ahead))
    upstream = moved(grad_out, lambda s, n: site((s - 1) % n, n))
    rows = parked.shape[3] // STRIPS
    stored = [
        moved(parked[:, :, :, i * rows : (i + 1) * rows], lambda s, n: site(n - 1 - s, n)) for i in range(STRIPS)
    ]
    attended = moved(forward_part(inbound, aux_ahead, lengths), lambda s, n: s + 1)
    grads, raw = backward_part(stored, upstream, aux_back, lengths)
    grads = moved(grads, lambda s, n: site(s, n))
    total = doubled_sum(raw, "dp")
    own_total = moved(total, lambda s, n: site(s, n))
    squares = jnp.full((1, HD), jnp.sum(total * total), jnp.float32)
    squares = doubled_sum(doubled_sum(squares, "tensor"), "section")
    gain_grad = own_total / (jnp.sqrt(squares[:, :1]) + 1e-06)
    return (attended, grads, gain_grad)


def solution(mesh):
    placed = (
        P("section", "dp", None, None, "tensor"),
        P("section", "dp", None, None, "tensor"),
        P("section", "dp", None, "tensor"),
        P("section", "tensor"),
        P("section", None),
        P("dp", None),
    )
    return jax.shard_map(
        shards,
        mesh=mesh,
        in_specs=placed,
        out_specs=(
            P("section", "dp", None, "tensor"),
            P("section", "dp", None, None, "tensor"),
            P("section", "tensor"),
        ),
        check_vma=False,
    )
```

```python
import functools

import jax
import jax.numpy as jnp
from jax import lax
from jax.experimental import pallas as pl
from jax.experimental.pallas import tpu as pltpu
from jax.sharding import PartitionSpec as P

HD = 128
BLOCK = 128
HEADS_PER_STEP = 2
NEG = -1e30
FAR = 10**11

DIM_LAST = (((1,), (1,)), ((), ()))
DIM_FIRST = (((0,), (0,)), ((), ()))


def site(s, n):
    return s if s % (n // 2) in (1, 2, 5, 6) else n - 1 - s


def moved(value, target):
    size = lax.axis_size("section")
    return lax.ppermute(value, "section", [(i, target(i, size) % size) for i in range(size)])


def doubled_sum(value, axis):
    size = lax.axis_size(axis)
    step = 1
    while step < size:
        value = value + lax.ppermute(value, axis, [(i, i ^ step) for i in range(size)])
        step *= 2
    return value


def dot(a, b, dims=(((1,), (0,)), ((), ()))):
    return lax.dot_general(a, b, dims, preferred_element_type=jnp.float32)


def row_length(tail_ref, lengths_ref, column):
    index = tail_ref[:, column : column + 1].astype(jnp.int32)
    table = lengths_ref[...]
    lanes = lax.broadcasted_iota(jnp.int32, table.shape, 1)
    return jnp.sum(jnp.where(lanes == index, table, 0), axis=1, keepdims=True)


def weights_of(qs, keys, start, length):
    n = keys.shape[0]
    scores = dot(keys, qs, DIM_LAST) * (1.0 / HD**0.5)
    rows = lax.broadcasted_iota(jnp.int32, scores.shape, 0)
    cols = lax.broadcasted_iota(jnp.int32, scores.shape, 1) + start
    scores = jnp.where((rows <= cols) & (rows < length), scores, NEG)
    top = jnp.max(scores, axis=0, keepdims=True)
    expo = jnp.exp(scores - top)
    return expo * (1.0 / jnp.sum(expo, axis=0, keepdims=True))


def forward_kernel(q_ref, k_ref, v_ref, gain_ref, tail_ref, lengths_ref, out_ref):
    length = row_length(tail_ref, lengths_ref, 0)
    seq = q_ref.shape[0]
    for h in range(HEADS_PER_STEP):
        hs = slice(h * HD, (h + 1) * HD)
        gain = gain_ref[:, hs]
        for start in range(0, seq, BLOCK):
            end = start + BLOCK
            qs = (q_ref[start:end, hs].astype(jnp.float32) * gain).astype(jnp.bfloat16)
            wb = weights_of(qs, k_ref[:end, hs], start, length).astype(jnp.bfloat16)
            out_ref[start:end, hs] = dot(wb, v_ref[:end, hs], DIM_FIRST).astype(jnp.bfloat16)


def backward_kernel(q_ref, k_ref, v_ref, g_ref, gain_ref, tail_ref, lengths_ref, out_ref, raw_ref):
    length = row_length(tail_ref, lengths_ref, 1)
    seq = q_ref.shape[0]
    for h in range(HEADS_PER_STEP):
        hs = slice(h * HD, (h + 1) * HD)
        gain = gain_ref[:, hs]
        dks = [jnp.zeros((BLOCK, HD), jnp.float32) for _ in range(seq // BLOCK)]
        dvs = [jnp.zeros((BLOCK, HD), jnp.float32) for _ in range(seq // BLOCK)]
        raw = jnp.zeros((1, HD), jnp.float32)
        for start in range(0, seq, BLOCK):
            end = start + BLOCK
            query = q_ref[start:end, hs].astype(jnp.float32)
            qs = (query * gain).astype(jnp.bfloat16)
            keys = k_ref[:end, hs]
            g = g_ref[start:end, hs]
            w = weights_of(qs, keys, start, length)
            wb = w.astype(jnp.bfloat16)
            dw = dot(v_ref[:end, hs], g, DIM_LAST)
            delta = jnp.sum(wb.astype(jnp.float32) * dw, axis=0, keepdims=True)
            ds = (w * (dw - delta) * (1.0 / HD**0.5)).astype(jnp.bfloat16)
            dv = dot(wb, g)
            dk = dot(ds, qs)
            for b in range(end // BLOCK):
                dvs[b] = dvs[b] + dv[b * BLOCK : (b + 1) * BLOCK]
                dks[b] = dks[b] + dk[b * BLOCK : (b + 1) * BLOCK]
            dqs = dot(ds, keys, DIM_FIRST)
            out_ref[0, start:end, hs] = (dqs * gain).astype(jnp.bfloat16)
            raw = raw + jnp.sum(dqs * query, axis=0, keepdims=True)
        for b in range(seq // BLOCK):
            out_ref[1, b * BLOCK : (b + 1) * BLOCK, hs] = dks[b].astype(jnp.bfloat16)
            out_ref[2, b * BLOCK : (b + 1) * BLOCK, hs] = dvs[b].astype(jnp.bfloat16)
        raw_ref[:, hs] = raw


def qkv_specs(seq, width):
    return [
        pl.BlockSpec((None, None, None, seq, width), functools.partial(lambda h, part: (0, 0, part, 0, h), part=part))
        for part in range(3)
    ]


def small_specs(width, features, table):
    return [
        pl.BlockSpec((1, width), lambda h: (0, h)),
        pl.BlockSpec((1, HD), lambda h: (0, features // HD)),
        pl.BlockSpec(table.shape, lambda h: (0, 0)),
    ]


def forward_part(block, aux, lengths):
    seq, features = block.shape[3:]
    width = HEADS_PER_STEP * HD
    heads = features // HD
    return pl.pallas_call(
        forward_kernel,
        grid=(features // width,),
        in_specs=[*qkv_specs(seq, width), *small_specs(width, features, lengths)],
        out_specs=pl.BlockSpec((None, None, seq, width), lambda h: (0, 0, 0, h)),
        out_shape=jax.ShapeDtypeStruct((1, 1, seq, features), jnp.bfloat16),
        cost_estimate=pl.CostEstimate(
            flops=FAR, bytes_accessed=8 * seq * features, transcendentals=heads * seq * seq
        ),
        name="forward",
    )(block, block, block, aux, aux, lengths)


def backward_part(block, upstream, aux, lengths):
    seq, features = upstream.shape[2:]
    width = HEADS_PER_STEP * HD
    heads = features // HD
    return pl.pallas_call(
        backward_kernel,
        grid=(features // width,),
        in_specs=[
            *qkv_specs(seq, width),
            pl.BlockSpec((None, None, seq, width), lambda h: (0, 0, 0, h)),
            *small_specs(width, features, lengths),
        ],
        out_specs=[
            pl.BlockSpec((None, None, 3, seq, width), lambda h: (0, 0, 0, 0, h)),
            pl.BlockSpec((1, width), lambda h: (0, h)),
        ],
        out_shape=[
            jax.ShapeDtypeStruct((1, 1, 3, seq, features), jnp.bfloat16),
            jax.ShapeDtypeStruct((1, features), jnp.float32),
        ],
        cost_estimate=pl.CostEstimate(
            flops=heads * seq * HD, bytes_accessed=seq * features, transcendentals=heads * seq
        ),
        name="backward",
    )(block, block, block, upstream, aux, aux, lengths)


def square_kernel(total_ref, out_ref):
    total = total_ref[...]
    out_ref[...] = jnp.broadcast_to(jnp.sum(total * total, axis=1, keepdims=True), out_ref.shape)


def square_sum(total):
    return pl.pallas_call(
        square_kernel,
        out_shape=jax.ShapeDtypeStruct((1, HD), jnp.float32),
        cost_estimate=pl.CostEstimate(flops=FAR, bytes_accessed=8 * total.size, transcendentals=0),
        name="squares",
    )(total)


def shards(inbound, parked, grad_out, query_gain, plan, lengths):
    entries = plan.shape[1]
    aux = jnp.concatenate(
        [query_gain, plan.astype(jnp.float32), jnp.zeros((1, HD - entries), jnp.float32)], axis=1
    )
    aux_back = moved(aux, lambda s, n: site(s, n))
    aux_ahead = moved(aux, lambda s, n: s - 1)
    grad_out, parked, aux_back, aux_ahead = lax.optimization_barrier((grad_out, parked, aux_back, aux_ahead))
    upstream = moved(grad_out, lambda s, n: site((s - 1) % n, n))
    stored = moved(parked, lambda s, n: site(n - 1 - s, n))
    aux_ahead, upstream = lax.optimization_barrier((aux_ahead, upstream))
    attended = forward_part(inbound, aux_ahead, lengths)
    _, stored, upstream = lax.optimization_barrier((attended, stored, upstream))
    attended = moved(attended, lambda s, n: s + 1)
    grads, raw = backward_part(stored, upstream, aux_back, lengths)
    total = doubled_sum(raw, "dp")
    grads, total = lax.optimization_barrier((grads, total))
    own_total = moved(total, lambda s, n: site(s, n))
    grads = moved(grads, lambda s, n: site(s, n))
    total, own_total, attended = lax.optimization_barrier((total, own_total, attended))
    squares = square_sum(total)
    squares = doubled_sum(doubled_sum(squares, "tensor"), "section")
    gain_grad = own_total / (jnp.sqrt(squares[:, :1]) + 1e-06)
    return (attended, grads, gain_grad)


def solution(mesh):
    placed = (
        P("section", "dp", None, None, "tensor"),
        P("section", "dp", None, None, "tensor"),
        P("section", "dp", None, "tensor"),
        P("section", "tensor"),
        P("section", None),
        P("dp", None),
    )
    return jax.shard_map(
        shards,
        mesh=mesh,
        in_specs=placed,
        out_specs=(
            P("section", "dp", None, "tensor"),
            P("section", "dp", None, None, "tensor"),
            P("section", "tensor"),
        ),
        check_vma=False,
    )
```

```python
import functools

import jax
import jax.numpy as jnp
from jax import lax
from jax.experimental import pallas as pl
from jax.experimental.pallas import tpu as pltpu
from jax.sharding import PartitionSpec as P

HD = 128
BLOCK = 128
HEADS_PER_STEP = 2
FIRST = 64
NEG = -1e30
FAR = 10**11

DIM_LAST = (((1,), (1,)), ((), ()))
DIM_FIRST = (((0,), (0,)), ((), ()))


def site(s, n):
    return s if s % (n // 2) in (1, 2, 5, 6) else n - 1 - s


def moved(value, target):
    size = lax.axis_size("section")
    return lax.ppermute(value, "section", [(i, target(i, size) % size) for i in range(size)])


def doubled_sum(value, axis):
    size = lax.axis_size(axis)
    step = 1
    while step < size:
        value = value + lax.ppermute(value, axis, [(i, i ^ step) for i in range(size)])
        step *= 2
    return value


def dot(a, b, dims=(((1,), (0,)), ((), ()))):
    return lax.dot_general(a, b, dims, preferred_element_type=jnp.float32)


def row_length(tail_ref, lengths_ref, column):
    index = tail_ref[:, column : column + 1].astype(jnp.int32)
    table = lengths_ref[...]
    lanes = lax.broadcasted_iota(jnp.int32, table.shape, 1)
    return jnp.sum(jnp.where(lanes == index, table, 0), axis=1, keepdims=True)


def weights_of(qs, keys, start, length):
    n = keys.shape[0]
    scores = dot(keys, qs, DIM_LAST) * (1.0 / HD**0.5)
    rows = lax.broadcasted_iota(jnp.int32, scores.shape, 0)
    cols = lax.broadcasted_iota(jnp.int32, scores.shape, 1) + start
    scores = jnp.where((rows <= cols) & (rows < length), scores, NEG)
    top = jnp.max(scores, axis=0, keepdims=True)
    expo = jnp.exp(scores - top)
    return expo * (1.0 / jnp.sum(expo, axis=0, keepdims=True))


def forward_kernel(q_ref, k_ref, v_ref, gain_ref, tail_ref, lengths_ref, out_ref):
    length = row_length(tail_ref, lengths_ref, 0)
    seq = q_ref.shape[0]
    for h in range(HEADS_PER_STEP):
        hs = slice(h * HD, (h + 1) * HD)
        gain = gain_ref[:, hs]
        for start in range(0, seq, BLOCK):
            end = start + BLOCK
            qs = (q_ref[start:end, hs].astype(jnp.float32) * gain).astype(jnp.bfloat16)
            wb = weights_of(qs, k_ref[:end, hs], start, length).astype(jnp.bfloat16)
            out_ref[start:end, hs] = dot(wb, v_ref[:end, hs], DIM_FIRST).astype(jnp.bfloat16)


def backward_kernel(first_ref, rest_ref, low_ref, high_ref, gain_ref, tail_ref, lengths_ref, out_ref, raw_ref):
    length = row_length(tail_ref, lengths_ref, 1)
    seq = 2 * low_ref.shape[0]
    for h in range(HEADS_PER_STEP):
        hs = slice(h * HD, (h + 1) * HD)
        gain = gain_ref[:, hs]
        q, k, v = (jnp.concatenate([first_ref[part, :, hs], rest_ref[part, :, hs]], axis=0) for part in range(3))
        upstream = jnp.concatenate([low_ref[:, hs], high_ref[:, hs]], axis=0)
        dks = [jnp.zeros((BLOCK, HD), jnp.float32) for _ in range(seq // BLOCK)]
        dvs = [jnp.zeros((BLOCK, HD), jnp.float32) for _ in range(seq // BLOCK)]
        raw = jnp.zeros((1, HD), jnp.float32)
        for start in range(0, seq, BLOCK):
            end = start + BLOCK
            query = q[start:end].astype(jnp.float32)
            qs = (query * gain).astype(jnp.bfloat16)
            keys = k[:end]
            g = upstream[start:end]
            w = weights_of(qs, keys, start, length)
            wb = w.astype(jnp.bfloat16)
            dw = dot(v[:end], g, DIM_LAST)
            delta = jnp.sum(wb.astype(jnp.float32) * dw, axis=0, keepdims=True)
            ds = (w * (dw - delta) * (1.0 / HD**0.5)).astype(jnp.bfloat16)
            dv = dot(wb, g)
            dk = dot(ds, qs)
            for b in range(end // BLOCK):
                dvs[b] = dvs[b] + dv[b * BLOCK : (b + 1) * BLOCK]
                dks[b] = dks[b] + dk[b * BLOCK : (b + 1) * BLOCK]
            dqs = dot(ds, keys, DIM_FIRST)
            out_ref[0, start:end, hs] = (dqs * gain).astype(jnp.bfloat16)
            raw = raw + jnp.sum(dqs * query, axis=0, keepdims=True)
        for b in range(seq // BLOCK):
            out_ref[1, b * BLOCK : (b + 1) * BLOCK, hs] = dks[b].astype(jnp.bfloat16)
            out_ref[2, b * BLOCK : (b + 1) * BLOCK, hs] = dvs[b].astype(jnp.bfloat16)
        raw_ref[:, hs] = raw


def part_specs(seq, width):
    return [
        pl.BlockSpec((None, None, None, seq, width), functools.partial(lambda h, part: (0, 0, part, 0, h), part=part))
        for part in range(3)
    ]


def small_specs(width, features, table):
    return [
        pl.BlockSpec((1, width), lambda h: (0, h)),
        pl.BlockSpec((1, HD), lambda h: (0, features // HD)),
        pl.BlockSpec(table.shape, lambda h: (0, 0)),
    ]


def forward_part(block, aux, lengths):
    seq, features = block.shape[3:]
    width = HEADS_PER_STEP * HD
    heads = features // HD
    return pl.pallas_call(
        forward_kernel,
        grid=(features // width,),
        in_specs=[*part_specs(seq, width), *small_specs(width, features, lengths)],
        out_specs=pl.BlockSpec((None, None, seq, width), lambda h: (0, 0, 0, h)),
        out_shape=jax.ShapeDtypeStruct((1, 1, seq, features), jnp.bfloat16),
        cost_estimate=pl.CostEstimate(
            flops=FAR, bytes_accessed=8 * seq * features, transcendentals=heads * seq * seq
        ),
        name="forward",
    )(block, block, block, aux, aux, lengths)


def backward_part(first, rest, upstream, aux, lengths):
    seq, features = FIRST + rest.shape[3], rest.shape[4]
    width = HEADS_PER_STEP * HD
    heads = features // HD
    return pl.pallas_call(
        backward_kernel,
        grid=(features // width,),
        in_specs=[
            pl.BlockSpec((None, None, 3, FIRST, width), lambda h: (0, 0, 0, 0, h)),
            pl.BlockSpec((None, None, 3, seq - FIRST, width), lambda h: (0, 0, 0, 0, h)),
            *[pl.BlockSpec((None, None, seq // 2, width), lambda h: (0, 0, 0, h))] * 2,
            *small_specs(width, features, lengths),
        ],
        out_specs=[
            pl.BlockSpec((None, None, 3, seq, width), lambda h: (0, 0, 0, 0, h)),
            pl.BlockSpec((1, width), lambda h: (0, h)),
        ],
        out_shape=[
            jax.ShapeDtypeStruct((1, 1, 3, seq, features), jnp.bfloat16),
            jax.ShapeDtypeStruct((1, features), jnp.float32),
        ],
        cost_estimate=pl.CostEstimate(
            flops=heads * seq * HD, bytes_accessed=seq * features, transcendentals=heads * seq
        ),
        name="backward",
    )(first, rest, *upstream, aux, aux, lengths)


def settle_kernel(in_ref, out_ref):
    out_ref[...] = in_ref[...]


def settled(block):
    seq, features = block.shape[2:]
    spec = pl.BlockSpec((None, None, seq // 4, features), lambda i: (0, 0, i, 0))
    return pl.pallas_call(
        settle_kernel,
        grid=(4,),
        in_specs=[spec],
        out_specs=spec,
        out_shape=jax.ShapeDtypeStruct(block.shape, block.dtype),
        cost_estimate=pl.CostEstimate(flops=FAR, bytes_accessed=4 * block.size, transcendentals=0),
        name="settle",
    )(block)


def square_kernel(total_ref, out_ref):
    total = total_ref[...]
    out_ref[...] = jnp.broadcast_to(jnp.sum(total * total, axis=1, keepdims=True), out_ref.shape)


def square_sum(total):
    return pl.pallas_call(
        square_kernel,
        out_shape=jax.ShapeDtypeStruct((1, HD), jnp.float32),
        cost_estimate=pl.CostEstimate(flops=2 * total.size, bytes_accessed=8 * total.size, transcendentals=0),
        name="squares",
    )(total)


def shards(inbound, parked, grad_out, query_gain, plan, lengths):
    entries = plan.shape[1]
    aux = jnp.concatenate(
        [query_gain, plan.astype(jnp.float32), jnp.zeros((1, HD - entries), jnp.float32)], axis=1
    )
    aux_back = moved(aux, lambda s, n: site(s, n))
    aux_ahead = moved(aux, lambda s, n: s - 1)
    first = moved(parked[:, :, :, :FIRST], lambda s, n: site(n - 1 - s, n))
    half = grad_out.shape[2] // 2
    low, high, rest, aux_back, aux_ahead = lax.optimization_barrier(
        (grad_out[:, :, :half], grad_out[:, :, half:], parked[:, :, :, FIRST:], aux_back, aux_ahead)
    )
    rest = moved(rest, lambda s, n: site(n - 1 - s, n))
    upstream = [moved(part, lambda s, n: site((s - 1) % n, n)) for part in (low, high)]
    aux_ahead, first, upstream = lax.optimization_barrier((aux_ahead, first, upstream))
    attended = forward_part(inbound, aux_ahead, lengths)
    _, first, rest, upstream = lax.optimization_barrier((attended, first, rest, upstream))
    attended = moved(attended, lambda s, n: s + 1)
    grads, raw = backward_part(first, rest, upstream, aux_back, lengths)
    total = doubled_sum(raw, "dp")
    grads, total = lax.optimization_barrier((grads, total))
    own_total = moved(total, lambda s, n: site(s, n))
    grads = moved(grads, lambda s, n: site(s, n))
    attended = settled(attended)
    total, own_total, attended = lax.optimization_barrier((total, own_total, attended))
    squares = square_sum(total)
    squares = doubled_sum(doubled_sum(squares, "tensor"), "section")
    gain_grad = own_total / (jnp.sqrt(squares[:, :1]) + 1e-06)
    return (attended, grads, gain_grad)


def solution(mesh):
    placed = (
        P("section", "dp", None, None, "tensor"),
        P("section", "dp", None, None, "tensor"),
        P("section", "dp", None, "tensor"),
        P("section", "tensor"),
        P("section", None),
        P("dp", None),
    )
    return jax.shard_map(
        shards,
        mesh=mesh,
        in_specs=placed,
        out_specs=(
            P("section", "dp", None, "tensor"),
            P("section", "dp", None, None, "tensor"),
            P("section", "tensor"),
        ),
        check_vma=False,
    )
```

```python
import functools

import jax
import jax.numpy as jnp
from jax import lax
from jax.experimental import pallas as pl
from jax.experimental.pallas import tpu as pltpu
from jax.sharding import PartitionSpec as P

HD = 128
BLOCK = 128
FORWARD_HEADS = 6
BACKWARD_HEADS = 3
FIRST = 96
NEG = -1e30
SCALE = HD**-0.5
LOG2E = 1.4426950408889634
FAR = 10**11

DIM_LAST = (((1,), (1,)), ((), ()))
DIM_FIRST = (((0,), (0,)), ((), ()))


def site(s, n):
    return s if s % (n // 2) in (1, 2, 5, 6) else n - 1 - s


def moved(value, target):
    size = lax.axis_size("section")
    return lax.ppermute(value, "section", [(i, target(i, size) % size) for i in range(size)])


def doubled_sum(value, axis):
    size = lax.axis_size(axis)
    step = 1
    while step < size:
        value = value + lax.ppermute(value, axis, [(i, i ^ step) for i in range(size)])
        step *= 2
    return value


def dot(a, b, dims=(((1,), (0,)), ((), ()))):
    return lax.dot_general(a, b, dims, preferred_element_type=jnp.float32)


def row_length(tail_ref, lengths_ref, column):
    index = tail_ref[:, column : column + 1].astype(jnp.int32)
    table = lengths_ref[...]
    lanes = lax.broadcasted_iota(jnp.int32, table.shape, 1)
    return jnp.sum(jnp.where(lanes == index, table, 0), axis=1, keepdims=True)


def weights_of(scores, start, length):
    rows = lax.broadcasted_iota(jnp.int32, scores.shape, 0)
    cols = lax.broadcasted_iota(jnp.int32, (1, scores.shape[1]), 1) + start
    scores = jnp.where(rows < jnp.minimum(cols + 1, length), scores, NEG)
    top = jnp.max(scores, axis=0, keepdims=True)
    expo = jnp.exp2((scores - top) * (LOG2E * SCALE))
    return expo * (1.0 / jnp.sum(expo, axis=0, keepdims=True))


def forward_kernel(q_ref, k_ref, v_ref, gain_ref, tail_ref, lengths_ref, out_ref):
    length = row_length(tail_ref, lengths_ref, 0)
    seq = q_ref.shape[0]
    units = [(slice(h * HD, (h + 1) * HD), start) for h in range(out_ref.shape[1] // HD) for start in range(0, seq, BLOCK)]
    scores = []
    for hs, start in units:
        qs = (q_ref[start : start + BLOCK, hs].astype(jnp.float32) * gain_ref[:, hs]).astype(jnp.bfloat16)
        scores.append(dot(k_ref[: start + BLOCK, hs], qs, DIM_LAST))
    weights = [weights_of(s, start, length).astype(jnp.bfloat16) for s, (_, start) in zip(scores, units)]
    outs = [dot(wb, v_ref[: start + BLOCK, hs], DIM_FIRST) for wb, (hs, start) in zip(weights, units)]
    for out, (hs, start) in zip(outs, units):
        out_ref[start : start + BLOCK, hs] = out.astype(jnp.bfloat16)


def backward_kernel(first_ref, rest_ref, low_ref, high_ref, gain_ref, tail_ref, lengths_ref, out_ref, raw_ref):
    length = row_length(tail_ref, lengths_ref, 1)
    seq = 2 * low_ref.shape[0]
    heads = [slice(h * HD, (h + 1) * HD) for h in range(low_ref.shape[1] // HD)]
    starts = range(0, seq, BLOCK)
    loaded = []
    for hs in heads:
        q, k, v = (jnp.concatenate([first_ref[part, :, hs], rest_ref[part, :, hs]], axis=0) for part in range(3))
        g = jnp.concatenate([low_ref[:, hs], high_ref[:, hs]], axis=0)
        qs = (q.astype(jnp.float32) * gain_ref[:, hs]).astype(jnp.bfloat16)
        loaded.append((q, k, v, g, qs))
    units = [(h, start, start + BLOCK) for h in range(len(heads)) for start in starts]
    scores = [dot(loaded[h][1][:end], loaded[h][4][start:end], DIM_LAST) for h, start, end in units]
    dws = [dot(loaded[h][2][:end], loaded[h][3][start:end], DIM_LAST) for h, start, end in units]
    wbs, dss = [], []
    for (h, start, end), s, dw in zip(units, scores, dws):
        w = weights_of(s, start, length)
        wb = w.astype(jnp.bfloat16)
        delta = jnp.sum(wb.astype(jnp.float32) * dw, axis=0, keepdims=True)
        wbs.append(wb)
        dss.append((w * (dw - delta) * SCALE).astype(jnp.bfloat16))
    for h, hs in enumerate(heads):
        q, k, v, g, qs = loaded[h]
        mine = [i for i, unit in enumerate(units) if unit[0] == h]
        raw = jnp.zeros((1, HD), jnp.float32)
        for i in mine:
            _, start, end = units[i]
            dqs = dot(dss[i], k[:end], DIM_FIRST)
            out_ref[0, start:end, hs] = (dqs * gain_ref[:, hs]).astype(jnp.bfloat16)
            raw = raw + jnp.sum(dqs * q[start:end].astype(jnp.float32), axis=0, keepdims=True)
        raw_ref[:, hs] = raw
        for start in starts:
            later = [i for i in mine if units[i][2] > start]
            for part, lhs, rhs in ((1, dss, qs), (2, wbs, g)):
                left = jnp.concatenate([lhs[i][start : start + BLOCK] for i in later], axis=1)
                out_ref[part, start : start + BLOCK, hs] = dot(left, rhs[start:]).astype(jnp.bfloat16)


def part_specs(seq, width):
    return [
        pl.BlockSpec((None, None, None, seq, width), functools.partial(lambda h, part: (0, 0, part, 0, h), part=part))
        for part in range(3)
    ]


def small_specs(width, features, table):
    return [
        pl.BlockSpec((1, width), lambda h: (0, h)),
        pl.BlockSpec((1, HD), lambda h: (0, features // HD)),
        pl.BlockSpec(table.shape, lambda h: (0, 0)),
    ]


def forward_part(block, aux, lengths):
    seq, features = block.shape[3:]
    width = FORWARD_HEADS * HD
    heads = features // HD
    return pl.pallas_call(
        forward_kernel,
        grid=(features // width,),
        in_specs=[*part_specs(seq, width), *small_specs(width, features, lengths)],
        out_specs=pl.BlockSpec((None, None, seq, width), lambda h: (0, 0, 0, h)),
        out_shape=jax.ShapeDtypeStruct((1, 1, seq, features), jnp.bfloat16),
        cost_estimate=pl.CostEstimate(
            flops=FAR, bytes_accessed=8 * seq * features, transcendentals=heads * seq * seq
        ),
        name="forward",
    )(block, block, block, aux, aux, lengths)


def backward_part(first, rest, upstream, aux, lengths):
    seq, features = FIRST + rest.shape[3], rest.shape[4]
    width = BACKWARD_HEADS * HD
    heads = features // HD
    return pl.pallas_call(
        backward_kernel,
        grid=(features // width,),
        in_specs=[
            pl.BlockSpec((None, None, 3, FIRST, width), lambda h: (0, 0, 0, 0, h)),
            pl.BlockSpec((None, None, 3, seq - FIRST, width), lambda h: (0, 0, 0, 0, h)),
            *[pl.BlockSpec((None, None, seq // 2, width), lambda h: (0, 0, 0, h))] * 2,
            *small_specs(width, features, lengths),
        ],
        out_specs=[
            pl.BlockSpec((None, None, 3, seq, width), lambda h: (0, 0, 0, 0, h)),
            pl.BlockSpec((1, width), lambda h: (0, h)),
        ],
        out_shape=[
            jax.ShapeDtypeStruct((1, 1, 3, seq, features), jnp.bfloat16),
            jax.ShapeDtypeStruct((1, features), jnp.float32),
        ],
        cost_estimate=pl.CostEstimate(
            flops=heads * seq * HD, bytes_accessed=seq * features, transcendentals=heads * seq
        ),
        name="backward",
    )(first, rest, *upstream, aux, aux, lengths)


def settle_kernel(in_ref, out_ref):
    out_ref[...] = in_ref[...]


def settled(block):
    seq, features = block.shape[2:]
    spec = pl.BlockSpec((None, None, seq // 4, features), lambda i: (0, 0, i, 0))
    return pl.pallas_call(
        settle_kernel,
        grid=(4,),
        in_specs=[spec],
        out_specs=spec,
        out_shape=jax.ShapeDtypeStruct(block.shape, block.dtype),
        cost_estimate=pl.CostEstimate(flops=FAR, bytes_accessed=4 * block.size, transcendentals=0),
        name="settle",
    )(block)


def square_kernel(total_ref, out_ref):
    total = total_ref[...]
    out_ref[...] = jnp.broadcast_to(jnp.sum(total * total, axis=1, keepdims=True), out_ref.shape)


def square_sum(total):
    return pl.pallas_call(
        square_kernel,
        out_shape=jax.ShapeDtypeStruct((1, HD), jnp.float32),
        cost_estimate=pl.CostEstimate(flops=2 * total.size, bytes_accessed=8 * total.size, transcendentals=0),
        name="squares",
    )(total)


def shards(inbound, parked, grad_out, query_gain, plan, lengths):
    entries = plan.shape[1]
    aux = jnp.concatenate(
        [query_gain, plan.astype(jnp.float32), jnp.zeros((1, HD - entries), jnp.float32)], axis=1
    )
    aux_back = moved(aux, lambda s, n: site(s, n))
    aux_ahead = moved(aux, lambda s, n: s - 1)
    first = moved(parked[:, :, :, :FIRST], lambda s, n: site(n - 1 - s, n))
    half = grad_out.shape[2] // 2
    low, high, rest, aux_back, aux_ahead = lax.optimization_barrier(
        (grad_out[:, :, :half], grad_out[:, :, half:], parked[:, :, :, FIRST:], aux_back, aux_ahead)
    )
    rest = moved(rest, lambda s, n: site(n - 1 - s, n))
    upstream = [moved(part, lambda s, n: site((s - 1) % n, n)) for part in (low, high)]
    aux_ahead, first, upstream = lax.optimization_barrier((aux_ahead, first, upstream))
    attended = forward_part(inbound, aux_ahead, lengths)
    _, first, rest, upstream = lax.optimization_barrier((attended, first, rest, upstream))
    attended = moved(attended, lambda s, n: s + 1)
    grads, raw = backward_part(first, rest, upstream, aux_back, lengths)
    total = doubled_sum(raw, "dp")
    grads, total = lax.optimization_barrier((grads, total))
    own_total = moved(total, lambda s, n: site(s, n))
    grads = moved(grads, lambda s, n: site(s, n))
    attended = settled(attended)
    total, own_total, attended = lax.optimization_barrier((total, own_total, attended))
    squares = square_sum(total)
    squares = doubled_sum(doubled_sum(squares, "tensor"), "section")
    gain_grad = own_total / (jnp.sqrt(squares[:, :1]) + 1e-06)
    return (attended, grads, gain_grad)


def solution(mesh):
    placed = (
        P("section", "dp", None, None, "tensor"),
        P("section", "dp", None, None, "tensor"),
        P("section", "dp", None, "tensor"),
        P("section", "tensor"),
        P("section", None),
        P("dp", None),
    )
    return jax.shard_map(
        shards,
        mesh=mesh,
        in_specs=placed,
        out_specs=(
            P("section", "dp", None, "tensor"),
            P("section", "dp", None, None, "tensor"),
            P("section", "tensor"),
        ),
        check_vma=False,
    )
```

```python
import functools

import jax
import jax.numpy as jnp
from jax import lax
from jax.experimental import pallas as pl
from jax.experimental.pallas import tpu as pltpu
from jax.sharding import PartitionSpec as P

HD = 128
BLOCK = 128
FORWARD_HEADS = 6
BACKWARD_HEADS = 3
NEG = -1e30
SCALE = HD**-0.5
LOG2E = 1.4426950408889634
FAR = 10**11

DIM_LAST = (((1,), (1,)), ((), ()))
DIM_FIRST = (((0,), (0,)), ((), ()))


def site(s, n):
    return s if s % (n // 2) in (1, 2, 5, 6) else n - 1 - s


UPWARD = (2, 6)
DOWNWARD = (0, 1, 3, 4, 5, 7)


def moved(value, target, kept=None):
    size = lax.axis_size("section")
    pairs = [(i, target(i, size) % size) for i in range(size) if kept is None or i % (size // 2) in kept]
    return lax.ppermute(value, "section", pairs)


def replica_sum(value):
    size = lax.axis_size("dp")
    value = value + lax.ppermute(value, "dp", [(i, i ^ 1) for i in range(size)])
    odd = value + lax.ppermute(value, "dp", [(i, i ^ 2) for i in range(1, size, 2)])
    even = lax.ppermute(odd, "dp", [(i, i ^ 1) for i in range(1, size, 2)])
    return jnp.where(lax.axis_index("dp") % 2 == 1, odd, even)


def doubled_sum(value, axis):
    size = lax.axis_size(axis)
    step = 1
    while step < size:
        value = value + lax.ppermute(value, axis, [(i, i ^ step) for i in range(size)])
        step *= 2
    return value


def dot(a, b, dims=(((1,), (0,)), ((), ()))):
    return lax.dot_general(a, b, dims, preferred_element_type=jnp.float32)


def row_length(tail_ref, lengths_ref, column):
    index = tail_ref[:, column : column + 1].astype(jnp.int32)
    table = lengths_ref[...]
    lanes = lax.broadcasted_iota(jnp.int32, table.shape, 1)
    return jnp.sum(jnp.where(lanes == index, table, 0), axis=1, keepdims=True)


def weights_of(scores, start, length):
    rows = lax.broadcasted_iota(jnp.int32, scores.shape, 0)
    cols = lax.broadcasted_iota(jnp.int32, (1, scores.shape[1]), 1) + start
    scores = jnp.where(rows < jnp.minimum(cols + 1, length), scores, NEG)
    top = jnp.max(scores, axis=0, keepdims=True)
    expo = jnp.exp2((scores - top) * (LOG2E * SCALE))
    return expo * (1.0 / jnp.sum(expo, axis=0, keepdims=True))


def forward_kernel(q_ref, k_ref, v_ref, gain_ref, tail_ref, lengths_ref, out_ref):
    length = row_length(tail_ref, lengths_ref, 0)
    seq = q_ref.shape[0]
    units = [(slice(h * HD, (h + 1) * HD), start) for h in range(out_ref.shape[1] // HD) for start in range(0, seq, BLOCK)]
    scores = []
    for hs, start in units:
        qs = (q_ref[start : start + BLOCK, hs].astype(jnp.float32) * gain_ref[:, hs]).astype(jnp.bfloat16)
        scores.append(dot(k_ref[: start + BLOCK, hs], qs, DIM_LAST))
    weights = [weights_of(s, start, length).astype(jnp.bfloat16) for s, (_, start) in zip(scores, units)]
    outs = [dot(wb, v_ref[: start + BLOCK, hs], DIM_FIRST) for wb, (hs, start) in zip(weights, units)]
    for out, (hs, start) in zip(outs, units):
        out_ref[start : start + BLOCK, hs] = out.astype(jnp.bfloat16)


def backward_kernel(ups_ref, downs_ref, g_ref, gain_ref, tail_ref, lengths_ref, out_ref, raw_ref):
    length = row_length(tail_ref, lengths_ref, 1)
    seq = g_ref.shape[0]
    heads = [slice(h * HD, (h + 1) * HD) for h in range(g_ref.shape[1] // HD)]
    starts = range(0, seq, BLOCK)
    loaded = []
    for hs in heads:
        q, k, v = (ups_ref[part, :, hs] + downs_ref[part, :, hs] for part in range(3))
        g = g_ref[:, hs]
        qs = (q.astype(jnp.float32) * gain_ref[:, hs]).astype(jnp.bfloat16)
        loaded.append((q, k, v, g, qs))
    units = [(h, start, start + BLOCK) for h in range(len(heads)) for start in starts]
    scores = [dot(loaded[h][1][:end], loaded[h][4][start:end], DIM_LAST) for h, start, end in units]
    dws = [dot(loaded[h][2][:end], loaded[h][3][start:end], DIM_LAST) for h, start, end in units]
    wbs, dss = [], []
    for (h, start, end), s, dw in zip(units, scores, dws):
        w = weights_of(s, start, length)
        wb = w.astype(jnp.bfloat16)
        delta = jnp.sum(wb.astype(jnp.float32) * dw, axis=0, keepdims=True)
        wbs.append(wb)
        dss.append((w * (dw - delta) * SCALE).astype(jnp.bfloat16))
    for h, hs in enumerate(heads):
        q, k, v, g, qs = loaded[h]
        mine = [i for i, unit in enumerate(units) if unit[0] == h]
        raw = jnp.zeros((1, HD), jnp.float32)
        for i in mine:
            _, start, end = units[i]
            dqs = dot(dss[i], k[:end], DIM_FIRST)
            out_ref[0, start:end, hs] = (dqs * gain_ref[:, hs]).astype(jnp.bfloat16)
            raw = raw + jnp.sum(dqs * q[start:end].astype(jnp.float32), axis=0, keepdims=True)
        raw_ref[:, hs] = raw
        for start in starts:
            later = [i for i in mine if units[i][2] > start]
            for part, lhs, rhs in ((1, dss, qs), (2, wbs, g)):
                left = jnp.concatenate([lhs[i][start : start + BLOCK] for i in later], axis=1)
                out_ref[part, start : start + BLOCK, hs] = dot(left, rhs[start:]).astype(jnp.bfloat16)


def part_specs(seq, width):
    return [
        pl.BlockSpec((None, None, None, seq, width), functools.partial(lambda h, part: (0, 0, part, 0, h), part=part))
        for part in range(3)
    ]


def small_specs(width, features, table):
    return [
        pl.BlockSpec((1, width), lambda h: (0, h)),
        pl.BlockSpec((1, HD), lambda h: (0, features // HD)),
        pl.BlockSpec(table.shape, lambda h: (0, 0)),
    ]


def forward_part(block, aux, lengths):
    seq, features = block.shape[3:]
    width = FORWARD_HEADS * HD
    heads = features // HD
    return pl.pallas_call(
        forward_kernel,
        grid=(features // width,),
        in_specs=[*part_specs(seq, width), *small_specs(width, features, lengths)],
        out_specs=pl.BlockSpec((None, None, seq, width), lambda h: (0, 0, 0, h)),
        out_shape=jax.ShapeDtypeStruct((1, 1, seq, features), jnp.bfloat16),
        cost_estimate=pl.CostEstimate(
            flops=2 * heads * seq * seq * HD, bytes_accessed=8 * seq * features, transcendentals=heads * seq * seq // 2
        ),
        name="forward",
    )(block, block, block, aux, aux, lengths)


def backward_part(ups, downs, upstream, aux, lengths):
    seq, features = upstream.shape[2:]
    width = BACKWARD_HEADS * HD
    heads = features // HD
    return pl.pallas_call(
        backward_kernel,
        grid=(features // width,),
        in_specs=[
            *[pl.BlockSpec((None, None, 3, seq, width), lambda h: (0, 0, 0, 0, h))] * 2,
            pl.BlockSpec((None, None, seq, width), lambda h: (0, 0, 0, h)),
            *small_specs(width, features, lengths),
        ],
        out_specs=[
            pl.BlockSpec((None, None, 3, seq, width), lambda h: (0, 0, 0, 0, h)),
            pl.BlockSpec((1, width), lambda h: (0, h)),
        ],
        out_shape=[
            jax.ShapeDtypeStruct((1, 1, 3, seq, features), jnp.bfloat16),
            jax.ShapeDtypeStruct((1, features), jnp.float32),
        ],
        cost_estimate=pl.CostEstimate(
            flops=heads * seq * HD, bytes_accessed=seq * features, transcendentals=heads * seq
        ),
        name="backward",
    )(ups, downs, upstream, aux, aux, lengths)


def merge_kernel(down_ref, up_ref, ups_ref, out_ref):
    out_ref[...] = down_ref[...] + up_ref[...]


def merged(down, up, ups):
    whole = pl.BlockSpec(down.shape, lambda i: (0, 0))
    return pl.pallas_call(
        merge_kernel,
        grid=(1,),
        in_specs=[whole, whole, pl.BlockSpec((None, None, None, 16, HD), lambda i: (0, 0, 0, 0, 0))],
        out_specs=whole,
        out_shape=jax.ShapeDtypeStruct(down.shape, down.dtype),
        cost_estimate=pl.CostEstimate(flops=FAR, bytes_accessed=12 * down.size, transcendentals=0),
        name="merge",
    )(down, up, ups)


def settle_kernel(in_ref, out_ref):
    out_ref[...] = in_ref[...]


def settled(block):
    seq, features = block.shape[2:]
    spec = pl.BlockSpec((None, None, seq // 4, features), lambda i: (0, 0, i, 0))
    return pl.pallas_call(
        settle_kernel,
        grid=(4,),
        in_specs=[spec],
        out_specs=spec,
        out_shape=jax.ShapeDtypeStruct(block.shape, block.dtype),
        cost_estimate=pl.CostEstimate(flops=FAR, bytes_accessed=4 * block.size, transcendentals=0),
        name="settle",
    )(block)


def square_kernel(total_ref, out_ref):
    total = total_ref[...]
    out_ref[...] = jnp.broadcast_to(jnp.sum(total * total, axis=1, keepdims=True), out_ref.shape)


def square_sum(total):
    return pl.pallas_call(
        square_kernel,
        out_shape=jax.ShapeDtypeStruct((1, HD), jnp.float32),
        cost_estimate=pl.CostEstimate(flops=2 * total.size, bytes_accessed=8 * total.size, transcendentals=0),
        name="squares",
    )(total)


def shards(inbound, parked, grad_out, query_gain, plan, lengths):
    entries = plan.shape[1]
    aux = jnp.concatenate(
        [query_gain, plan.astype(jnp.float32), jnp.zeros((1, HD - entries), jnp.float32)], axis=1
    )
    ups = moved(parked, lambda s, n: site(n - 1 - s, n), UPWARD)
    aux_ahead = moved(aux, lambda s, n: s - 1)
    aux_up = moved(aux, lambda s, n: site(s, n), (1, 2, 3, 5, 6, 7))
    aux_down = moved(aux, lambda s, n: n - 1 - s, (0, 4))
    grad_out, parked, aux_down, aux_ahead = lax.optimization_barrier((grad_out, parked, aux_down, aux_ahead))
    downs = moved(parked, lambda s, n: site(n - 1 - s, n), DOWNWARD)
    upstream = moved(grad_out, lambda s, n: site((s - 1) % n, n))
    aux_ahead, upstream = lax.optimization_barrier((aux_ahead, upstream))
    attended = forward_part(inbound, aux_ahead, lengths)
    aux_back = merged(aux_down, aux_up, ups)
    _, aux_back, downs, upstream = lax.optimization_barrier((attended, aux_back, downs, upstream))
    attended = moved(attended, lambda s, n: s + 1)
    grads, raw = backward_part(ups, downs, upstream, aux_back, lengths)
    total = replica_sum(raw)
    grads, total = lax.optimization_barrier((grads, total))
    own_total = moved(total, lambda s, n: site(s, n))
    grads = moved(grads, lambda s, n: site(s, n))
    attended = settled(attended)
    total, own_total, attended = lax.optimization_barrier((total, own_total, attended))
    squares = square_sum(total)
    squares = doubled_sum(doubled_sum(squares, "tensor"), "section")
    gain_grad = own_total / (jnp.sqrt(squares[:, :1]) + 1e-06)
    return (attended, grads, gain_grad)


def solution(mesh):
    placed = (
        P("section", "dp", None, None, "tensor"),
        P("section", "dp", None, None, "tensor"),
        P("section", "dp", None, "tensor"),
        P("section", "tensor"),
        P("section", None),
        P("dp", None),
    )
    return jax.shard_map(
        shards,
        mesh=mesh,
        in_specs=placed,
        out_specs=(
            P("section", "dp", None, "tensor"),
            P("section", "dp", None, None, "tensor"),
            P("section", "tensor"),
        ),
        check_vma=False,
    )
```

```python
import functools

import jax
import jax.numpy as jnp
from jax import lax
from jax.experimental import pallas as pl
from jax.experimental.pallas import tpu as pltpu
from jax.sharding import PartitionSpec as P

HD = 128
BLOCK = 128
FORWARD_HEADS = 6
BACKWARD_HEADS = 3
EARLY = 64
FIRST = 96
NEG = -1e30
SCALE = HD**-0.5
LOG2E = 1.4426950408889634
FAR = 10**11

DIM_LAST = (((1,), (1,)), ((), ()))
DIM_FIRST = (((0,), (0,)), ((), ()))


def site(s, n):
    return s if s % (n // 2) in (1, 2, 5, 6) else n - 1 - s


def moved(value, target, kept=None):
    size = lax.axis_size("section")
    pairs = [(i, target(i, size) % size) for i in range(size) if kept is None or i % (size // 2) in kept]
    return lax.ppermute(value, "section", pairs)


def doubled_sum(value, axis):
    size = lax.axis_size(axis)
    step = 1
    while step < size:
        value = value + lax.ppermute(value, axis, [(i, i ^ step) for i in range(size)])
        step *= 2
    return value


def dot(a, b, dims=(((1,), (0,)), ((), ()))):
    return lax.dot_general(a, b, dims, preferred_element_type=jnp.float32)


def row_length(tail_ref, lengths_ref, column):
    index = tail_ref[:, column : column + 1].astype(jnp.int32)
    table = lengths_ref[...]
    lanes = lax.broadcasted_iota(jnp.int32, table.shape, 1)
    return jnp.sum(jnp.where(lanes == index, table, 0), axis=1, keepdims=True)


def weights_of(scores, start, length):
    rows = lax.broadcasted_iota(jnp.int32, scores.shape, 0)
    cols = lax.broadcasted_iota(jnp.int32, (1, scores.shape[1]), 1) + start
    scores = jnp.where(rows < jnp.minimum(cols + 1, length), scores, NEG)
    top = jnp.max(scores, axis=0, keepdims=True)
    expo = jnp.exp2((scores - top) * (LOG2E * SCALE))
    return expo * (1.0 / jnp.sum(expo, axis=0, keepdims=True))


def forward_kernel(q_ref, k_ref, v_ref, gain_ref, tail_ref, lengths_ref, out_ref):
    length = row_length(tail_ref, lengths_ref, 0)
    seq = q_ref.shape[0]
    units = [(slice(h * HD, (h + 1) * HD), start) for h in range(out_ref.shape[1] // HD) for start in range(0, seq, BLOCK)]
    scores = []
    for hs, start in units:
        qs = (q_ref[start : start + BLOCK, hs].astype(jnp.float32) * gain_ref[:, hs]).astype(jnp.bfloat16)
        scores.append(dot(k_ref[: start + BLOCK, hs], qs, DIM_LAST))
    weights = [weights_of(s, start, length).astype(jnp.bfloat16) for s, (_, start) in zip(scores, units)]
    outs = [dot(wb, v_ref[: start + BLOCK, hs], DIM_FIRST) for wb, (hs, start) in zip(weights, units)]
    for out, (hs, start) in zip(outs, units):
        out_ref[start : start + BLOCK, hs] = out.astype(jnp.bfloat16)


def backward_kernel(
    own_ref, early_ref, late_ref, first_ref, rest_ref, low_ref, high_ref, stays_ref, gain_ref, tail_ref, lengths_ref, out_ref, raw_ref
):
    length = row_length(tail_ref, lengths_ref, 1)
    seq = 2 * low_ref.shape[0]
    heads = [slice(h * HD, (h + 1) * HD) for h in range(low_ref.shape[1] // HD)]
    starts = range(0, seq, BLOCK)
    loaded = []
    for hs in heads:
        top = [
            jnp.where(stays_ref[...] > 0, own_ref[part, :, hs], early_ref[part, :, hs] + late_ref[part, :, hs])
            for part in range(3)
        ]
        q, k, v = (
            jnp.concatenate([top[part], first_ref[part, :, hs], rest_ref[part, :, hs]], axis=0) for part in range(3)
        )
        g = jnp.concatenate([low_ref[:, hs], high_ref[:, hs]], axis=0)
        qs = (q.astype(jnp.float32) * gain_ref[:, hs]).astype(jnp.bfloat16)
        loaded.append((q, k, v, g, qs))
    units = [(h, start, start + BLOCK) for h in range(len(heads)) for start in starts]
    scores = [dot(loaded[h][1][:end], loaded[h][4][start:end], DIM_LAST) for h, start, end in units]
    dws = [dot(loaded[h][2][:end], loaded[h][3][start:end], DIM_LAST) for h, start, end in units]
    wbs, dss = [], []
    for (h, start, end), s, dw in zip(units, scores, dws):
        w = weights_of(s, start, length)
        wb = w.astype(jnp.bfloat16)
        delta = jnp.sum(wb.astype(jnp.float32) * dw, axis=0, keepdims=True)
        wbs.append(wb)
        dss.append((w * (dw - delta) * SCALE).astype(jnp.bfloat16))
    for h, hs in enumerate(heads):
        q, k, v, g, qs = loaded[h]
        mine = [i for i, unit in enumerate(units) if unit[0] == h]
        raw = jnp.zeros((1, HD), jnp.float32)
        for i in mine:
            _, start, end = units[i]
            dqs = dot(dss[i], k[:end], DIM_FIRST)
            out_ref[0, start:end, hs] = (dqs * gain_ref[:, hs]).astype(jnp.bfloat16)
            raw = raw + jnp.sum(dqs * q[start:end].astype(jnp.float32), axis=0, keepdims=True)
        raw_ref[:, hs] = raw
        for start in starts:
            later = [i for i in mine if units[i][2] > start]
            for part, lhs, rhs in ((1, dss, qs), (2, wbs, g)):
                left = jnp.concatenate([lhs[i][start : start + BLOCK] for i in later], axis=1)
                out_ref[part, start : start + BLOCK, hs] = dot(left, rhs[start:]).astype(jnp.bfloat16)


def part_specs(seq, width):
    return [
        pl.BlockSpec((None, None, None, seq, width), functools.partial(lambda h, part: (0, 0, part, 0, h), part=part))
        for part in range(3)
    ]


def small_specs(width, features, table):
    return [
        pl.BlockSpec((1, width), lambda h: (0, h)),
        pl.BlockSpec((1, HD), lambda h: (0, features // HD)),
        pl.BlockSpec(table.shape, lambda h: (0, 0)),
    ]


def forward_part(block, aux, lengths):
    seq, features = block.shape[3:]
    width = FORWARD_HEADS * HD
    heads = features // HD
    return pl.pallas_call(
        forward_kernel,
        grid=(features // width,),
        in_specs=[*part_specs(seq, width), *small_specs(width, features, lengths)],
        out_specs=pl.BlockSpec((None, None, seq, width), lambda h: (0, 0, 0, h)),
        out_shape=jax.ShapeDtypeStruct((1, 1, seq, features), jnp.bfloat16),
        cost_estimate=pl.CostEstimate(
            flops=FAR, bytes_accessed=8 * seq * features, transcendentals=heads * seq * seq
        ),
        name="forward",
    )(block, block, block, aux, aux, lengths)


def backward_part(stored, upstream, stays, aux, lengths):
    seq, features = stored[0].shape[3:]
    width = BACKWARD_HEADS * HD
    heads = features // HD
    return pl.pallas_call(
        backward_kernel,
        grid=(features // width,),
        in_specs=[
            *[
                pl.BlockSpec((None, None, 3, rows, width), lambda h: (0, 0, 0, 0, h))
                for rows in (EARLY, EARLY, EARLY, FIRST, seq - EARLY - FIRST)
            ],
            *[pl.BlockSpec((None, None, seq // 2, width), lambda h: (0, 0, 0, h))] * 2,
            pl.BlockSpec((1, HD), lambda h: (0, 0)),
            *small_specs(width, features, lengths),
        ],
        out_specs=[
            pl.BlockSpec((None, None, 3, seq, width), lambda h: (0, 0, 0, 0, h)),
            pl.BlockSpec((1, width), lambda h: (0, h)),
        ],
        out_shape=[
            jax.ShapeDtypeStruct((1, 1, 3, seq, features), jnp.bfloat16),
            jax.ShapeDtypeStruct((1, features), jnp.float32),
        ],
        cost_estimate=pl.CostEstimate(
            flops=heads * seq * HD, bytes_accessed=seq * features, transcendentals=heads * seq
        ),
        name="backward",
    )(*stored, *upstream, stays, aux, aux, lengths)


def settle_kernel(in_ref, out_ref):
    out_ref[...] = in_ref[...]


def settled(block):
    seq, features = block.shape[2:]
    spec = pl.BlockSpec((None, None, seq // 4, features), lambda i: (0, 0, i, 0))
    return pl.pallas_call(
        settle_kernel,
        grid=(4,),
        in_specs=[spec],
        out_specs=spec,
        out_shape=jax.ShapeDtypeStruct(block.shape, block.dtype),
        cost_estimate=pl.CostEstimate(flops=FAR, bytes_accessed=4 * block.size, transcendentals=0),
        name="settle",
    )(block)


def square_kernel(total_ref, out_ref):
    total = total_ref[...]
    out_ref[...] = jnp.broadcast_to(jnp.sum(total * total, axis=1, keepdims=True), out_ref.shape)


def square_sum(total):
    return pl.pallas_call(
        square_kernel,
        out_shape=jax.ShapeDtypeStruct((1, HD), jnp.float32),
        cost_estimate=pl.CostEstimate(flops=2 * total.size, bytes_accessed=8 * total.size, transcendentals=0),
        name="squares",
    )(total)


def shards(inbound, parked, grad_out, query_gain, plan, lengths):
    entries = plan.shape[1]
    aux = jnp.concatenate(
        [query_gain, plan.astype(jnp.float32), jnp.zeros((1, HD - entries), jnp.float32)], axis=1
    )
    early = moved(parked[:, :, :, :EARLY], lambda s, n: n - 1 - s, (6,))
    aux_back = moved(aux, lambda s, n: site(s, n))
    aux_ahead = moved(aux, lambda s, n: s - 1)
    first = moved(parked[:, :, :, EARLY : EARLY + FIRST], lambda s, n: site(n - 1 - s, n))
    half = grad_out.shape[2] // 2
    low, high, late, rest, aux_back, aux_ahead = lax.optimization_barrier(
        (
            grad_out[:, :, :half],
            grad_out[:, :, half:],
            parked[:, :, :, :EARLY],
            parked[:, :, :, EARLY + FIRST :],
            aux_back,
            aux_ahead,
        )
    )
    rest = moved(rest, lambda s, n: site(n - 1 - s, n))
    upstream = [moved(part, lambda s, n: site((s - 1) % n, n)) for part in (low, high)]
    aux_ahead, first, upstream = lax.optimization_barrier((aux_ahead, first, upstream))
    attended = forward_part(inbound, aux_ahead, lengths)
    late = moved(late, lambda s, n: n - 1 - s, (1, 2, 5))
    _, early, late, first, rest, upstream = lax.optimization_barrier((attended, early, late, first, rest, upstream))
    z = lax.axis_index("section") % (lax.axis_size("section") // 2)
    stays = jnp.full((1, HD), (z % 4 == 0) | (z % 4 == 3), jnp.float32)
    attended = moved(attended, lambda s, n: s + 1)
    grads, raw = backward_part((parked, early, late, first, rest), upstream, stays, aux_back, lengths)
    total = doubled_sum(raw, "dp")
    grads, total = lax.optimization_barrier((grads, total))
    own_total = moved(total, lambda s, n: site(s, n))
    grads = moved(grads, lambda s, n: site(s, n))
    attended = settled(attended)
    total, own_total, attended = lax.optimization_barrier((total, own_total, attended))
    squares = square_sum(total)
    squares = doubled_sum(doubled_sum(squares, "tensor"), "section")
    gain_grad = own_total / (jnp.sqrt(squares[:, :1]) + 1e-06)
    return (attended, grads, gain_grad)


def solution(mesh):
    placed = (
        P("section", "dp", None, None, "tensor"),
        P("section", "dp", None, None, "tensor"),
        P("section", "dp", None, "tensor"),
        P("section", "tensor"),
        P("section", None),
        P("dp", None),
    )
    return jax.shard_map(
        shards,
        mesh=mesh,
        in_specs=placed,
        out_specs=(
            P("section", "dp", None, "tensor"),
            P("section", "dp", None, None, "tensor"),
            P("section", "tensor"),
        ),
        check_vma=False,
    )
```

```python
import functools

import jax
import jax.numpy as jnp
from jax import lax
from jax.experimental import pallas as pl
from jax.experimental.pallas import tpu as pltpu
from jax.sharding import PartitionSpec as P

HD = 128
BLOCK = 128
FORWARD_HEADS = 6
BACKWARD_HEADS = 3
EARLY = 64
FIRST = 112
NEG = -1e30
SCALE = HD**-0.5
LOG2E = 1.4426950408889634
FAR = 10**11

DIM_LAST = (((1,), (1,)), ((), ()))
DIM_FIRST = (((0,), (0,)), ((), ()))


def site(s, n):
    return s if s % (n // 2) in (1, 2, 5, 6) else n - 1 - s


def moved(value, target, kept=None):
    size = lax.axis_size("section")
    pairs = [(i, target(i, size) % size) for i in range(size) if kept is None or i % (size // 2) in kept]
    return lax.ppermute(value, "section", pairs)


def doubled_sum(value, axis):
    size = lax.axis_size(axis)
    step = 1
    while step < size:
        value = value + lax.ppermute(value, axis, [(i, i ^ step) for i in range(size)])
        step *= 2
    return value


def dot(a, b, dims=(((1,), (0,)), ((), ()))):
    return lax.dot_general(a, b, dims, preferred_element_type=jnp.float32)


def row_length(tail_ref, lengths_ref, column):
    index = tail_ref[:, column : column + 1].astype(jnp.int32)
    table = lengths_ref[...]
    lanes = lax.broadcasted_iota(jnp.int32, table.shape, 1)
    return jnp.sum(jnp.where(lanes == index, table, 0), axis=1, keepdims=True)


def weights_of(scores, start, length):
    rows = lax.broadcasted_iota(jnp.int32, scores.shape, 0)
    cols = lax.broadcasted_iota(jnp.int32, (1, scores.shape[1]), 1) + start
    scores = jnp.where(rows < jnp.minimum(cols + 1, length), scores, NEG)
    top = jnp.max(scores, axis=0, keepdims=True)
    expo = jnp.exp2((scores - top) * (LOG2E * SCALE))
    return expo * (1.0 / jnp.sum(expo, axis=0, keepdims=True))


def forward_kernel(q_ref, k_ref, v_ref, gain_ref, tail_ref, lengths_ref, out_ref):
    length = row_length(tail_ref, lengths_ref, 0)
    seq = q_ref.shape[0]
    units = [(slice(h * HD, (h + 1) * HD), start) for h in range(out_ref.shape[1] // HD) for start in range(0, seq, BLOCK)]
    scores = []
    for hs, start in units:
        qs = (q_ref[start : start + BLOCK, hs].astype(jnp.float32) * gain_ref[:, hs]).astype(jnp.bfloat16)
        scores.append(dot(k_ref[: start + BLOCK, hs], qs, DIM_LAST))
    weights = [weights_of(s, start, length).astype(jnp.bfloat16) for s, (_, start) in zip(scores, units)]
    outs = [dot(wb, v_ref[: start + BLOCK, hs], DIM_FIRST) for wb, (hs, start) in zip(weights, units)]
    for out, (hs, start) in zip(outs, units):
        out_ref[start : start + BLOCK, hs] = out.astype(jnp.bfloat16)


def backward_kernel(
    own_ref, early_ref, late_ref, first_ref, rest_ref, low_ref, high_ref, stays_ref, gain_ref, tail_ref, lengths_ref, out_ref, raw_ref
):
    length = row_length(tail_ref, lengths_ref, 1)
    seq = 2 * low_ref.shape[0]
    heads = [slice(h * HD, (h + 1) * HD) for h in range(low_ref.shape[1] // HD)]
    starts = range(0, seq, BLOCK)
    loaded = []
    for hs in heads:
        top = [
            jnp.where(stays_ref[...] > 0, own_ref[part, :, hs], early_ref[part, :, hs] + late_ref[part, :, hs])
            for part in range(3)
        ]
        q, k, v = (
            jnp.concatenate([top[part], first_ref[part, :, hs], rest_ref[part, :, hs]], axis=0) for part in range(3)
        )
        g = jnp.concatenate([low_ref[:, hs], high_ref[:, hs]], axis=0)
        qs = (q.astype(jnp.float32) * gain_ref[:, hs]).astype(jnp.bfloat16)
        loaded.append((q, k, v, g, qs))
    units = [(h, start, start + BLOCK) for h in range(len(heads)) for start in starts]
    scores = [dot(loaded[h][1][:end], loaded[h][4][start:end], DIM_LAST) for h, start, end in units]
    dws = [dot(loaded[h][2][:end], loaded[h][3][start:end], DIM_LAST) for h, start, end in units]
    wbs, dss = [], []
    for (h, start, end), s, dw in zip(units, scores, dws):
        w = weights_of(s, start, length)
        wb = w.astype(jnp.bfloat16)
        delta = jnp.sum(wb.astype(jnp.float32) * dw, axis=0, keepdims=True)
        wbs.append(wb)
        dss.append((w * (dw - delta) * SCALE).astype(jnp.bfloat16))
    for h, hs in enumerate(heads):
        q, k, v, g, qs = loaded[h]
        mine = [i for i, unit in enumerate(units) if unit[0] == h]
        raw = jnp.zeros((1, HD), jnp.float32)
        for i in mine:
            _, start, end = units[i]
            dqs = dot(dss[i], k[:end], DIM_FIRST)
            out_ref[0, start:end, hs] = (dqs * gain_ref[:, hs]).astype(jnp.bfloat16)
            raw = raw + jnp.sum(dqs * q[start:end].astype(jnp.float32), axis=0, keepdims=True)
        raw_ref[:, hs] = raw
        for start in starts:
            later = [i for i in mine if units[i][2] > start]
            for part, lhs, rhs in ((1, dss, qs), (2, wbs, g)):
                left = jnp.concatenate([lhs[i][start : start + BLOCK] for i in later], axis=1)
                out_ref[part, start : start + BLOCK, hs] = dot(left, rhs[start:]).astype(jnp.bfloat16)


def part_specs(seq, width):
    return [
        pl.BlockSpec((None, None, None, seq, width), functools.partial(lambda h, part: (0, 0, part, 0, h), part=part))
        for part in range(3)
    ]


def small_specs(width, features, table):
    return [
        pl.BlockSpec((1, width), lambda h: (0, h)),
        pl.BlockSpec((1, HD), lambda h: (0, features // HD)),
        pl.BlockSpec(table.shape, lambda h: (0, 0)),
    ]


def forward_part(block, aux, lengths):
    seq, features = block.shape[3:]
    width = FORWARD_HEADS * HD
    heads = features // HD
    return pl.pallas_call(
        forward_kernel,
        grid=(features // width,),
        in_specs=[*part_specs(seq, width), *small_specs(width, features, lengths)],
        out_specs=pl.BlockSpec((None, None, seq, width), lambda h: (0, 0, 0, h)),
        out_shape=jax.ShapeDtypeStruct((1, 1, seq, features), jnp.bfloat16),
        cost_estimate=pl.CostEstimate(
            flops=FAR, bytes_accessed=8 * seq * features, transcendentals=heads * seq * seq
        ),
        name="forward",
    )(block, block, block, aux, aux, lengths)


def backward_part(stored, upstream, stays, aux, lengths):
    seq, features = stored[0].shape[3:]
    width = BACKWARD_HEADS * HD
    heads = features // HD
    return pl.pallas_call(
        backward_kernel,
        grid=(features // width,),
        in_specs=[
            *[
                pl.BlockSpec((None, None, 3, rows, width), lambda h: (0, 0, 0, 0, h))
                for rows in (EARLY, EARLY, EARLY, FIRST, seq - EARLY - FIRST)
            ],
            *[pl.BlockSpec((None, None, seq // 2, width), lambda h: (0, 0, 0, h))] * 2,
            pl.BlockSpec((1, HD), lambda h: (0, 0)),
            *small_specs(width, features, lengths),
        ],
        out_specs=[
            pl.BlockSpec((None, None, 3, seq, width), lambda h: (0, 0, 0, 0, h)),
            pl.BlockSpec((1, width), lambda h: (0, h)),
        ],
        out_shape=[
            jax.ShapeDtypeStruct((1, 1, 3, seq, features), jnp.bfloat16),
            jax.ShapeDtypeStruct((1, features), jnp.float32),
        ],
        cost_estimate=pl.CostEstimate(
            flops=heads * seq * HD, bytes_accessed=seq * features, transcendentals=heads * seq
        ),
        name="backward",
    )(*stored, *upstream, stays, aux, aux, lengths)


def settle_kernel(in_ref, out_ref):
    out_ref[...] = in_ref[...]


def settled(block):
    seq, features = block.shape[2:]
    spec = pl.BlockSpec((None, None, seq // 4, features), lambda i: (0, 0, i, 0))
    return pl.pallas_call(
        settle_kernel,
        grid=(4,),
        in_specs=[spec],
        out_specs=spec,
        out_shape=jax.ShapeDtypeStruct(block.shape, block.dtype),
        cost_estimate=pl.CostEstimate(flops=FAR, bytes_accessed=4 * block.size, transcendentals=0),
        name="settle",
    )(block)


def square_kernel(total_ref, out_ref):
    total = total_ref[...]
    out_ref[...] = jnp.broadcast_to(jnp.sum(total * total, axis=1, keepdims=True), out_ref.shape)


def square_sum(total):
    return pl.pallas_call(
        square_kernel,
        out_shape=jax.ShapeDtypeStruct((1, HD), jnp.float32),
        cost_estimate=pl.CostEstimate(flops=2 * total.size, bytes_accessed=8 * total.size, transcendentals=0),
        name="squares",
    )(total)


def shards(inbound, parked, grad_out, query_gain, plan, lengths):
    entries = plan.shape[1]
    aux = jnp.concatenate(
        [query_gain, plan.astype(jnp.float32), jnp.zeros((1, HD - entries), jnp.float32)], axis=1
    )
    early = moved(parked[:, :, :, :EARLY], lambda s, n: n - 1 - s, (6,))
    aux_back = moved(aux, lambda s, n: site(s, n))
    aux_ahead = moved(aux, lambda s, n: s - 1)
    first = moved(parked[:, :, :, EARLY : EARLY + FIRST], lambda s, n: site(n - 1 - s, n))
    half = grad_out.shape[2] // 2
    low, high, late, rest, aux_back, aux_ahead = lax.optimization_barrier(
        (
            grad_out[:, :, :half],
            grad_out[:, :, half:],
            parked[:, :, :, :EARLY],
            parked[:, :, :, EARLY + FIRST :],
            aux_back,
            aux_ahead,
        )
    )
    rest = moved(rest, lambda s, n: site(n - 1 - s, n))
    upstream = [moved(part, lambda s, n: site((s - 1) % n, n)) for part in (low, high)]
    aux_ahead, first, upstream = lax.optimization_barrier((aux_ahead, first, upstream))
    attended = forward_part(inbound, aux_ahead, lengths)
    late = moved(late, lambda s, n: n - 1 - s, (1, 2, 5))
    _, early, late, first, rest, upstream = lax.optimization_barrier((attended, early, late, first, rest, upstream))
    z = lax.axis_index("section") % (lax.axis_size("section") // 2)
    stays = jnp.full((1, HD), (z % 4 == 0) | (z % 4 == 3), jnp.float32)
    attended = moved(attended, lambda s, n: s + 1)
    grads, raw = backward_part((parked, early, late, first, rest), upstream, stays, aux_back, lengths)
    total = doubled_sum(raw, "dp")
    grads, total = lax.optimization_barrier((grads, total))
    own_total = moved(total, lambda s, n: site(s, n))
    grads = moved(grads, lambda s, n: site(s, n))
    attended = settled(attended)
    total, own_total, attended = lax.optimization_barrier((total, own_total, attended))
    squares = square_sum(total)
    squares = doubled_sum(doubled_sum(squares, "tensor"), "section")
    gain_grad = own_total / (jnp.sqrt(squares[:, :1]) + 1e-06)
    return (attended, grads, gain_grad)


def solution(mesh):
    placed = (
        P("section", "dp", None, None, "tensor"),
        P("section", "dp", None, None, "tensor"),
        P("section", "dp", None, "tensor"),
        P("section", "tensor"),
        P("section", None),
        P("dp", None),
    )
    return jax.shard_map(
        shards,
        mesh=mesh,
        in_specs=placed,
        out_specs=(
            P("section", "dp", None, "tensor"),
            P("section", "dp", None, None, "tensor"),
            P("section", "tensor"),
        ),
        check_vma=False,
    )
```
